256 devices in a mesh: branch: 4 (over y_lo, core), seq: 64 (over x, y_hi, z).
Axes of the slice: x: 4, y: 4 (y_hi: 2, y_lo: 2; y = y_hi * 2 + y_lo), z: 8, core: 2. Of those that a mesh axis runs over, the one named last changes fastest.
Arguments:
- ctrl_q: bfloat16 [4, 4096, 2048], P('branch', 'seq'), may hold values from -128 to 128
- ctrl_k: bfloat16 [4, 4096, 2048], P('branch', 'seq'), may hold values from -128 to 128
- ctrl_v: bfloat16 [4, 4096, 2048], P('branch', 'seq'), may hold values from -96 to 96
- joining_codes: int32 [4, 4096], P('branch', 'seq'), may hold values from 0 to 32
- base_q: bfloat16 [4096, 2048], P('seq', 'branch'), may hold values from -128 to 128
- base_k: bfloat16 [4096, 2048], P('seq', 'branch'), may hold values from -128 to 128
- base_v: bfloat16 [4096, 2048], P('seq', 'branch'), may hold values from -48 to 48
Outputs:
- joined: float32 [4096, 2048], P('seq', 'branch')
- base_out: bfloat16 [4096, 2048], P('seq', 'branch')
The draws below stay inside these ranges and needn't reach their ends.
All inputs are finite; a program needn't handle non-finite values.
Results may differ from the reference program's by a relative error of at most 0.013.
Values may be sent and summed in bfloat16 or wider, within the bound.
No kernel may reach another device: no remote copies, remote signals or barrier semaphores. Data moves between devices by JAX's collectives and lax.ppermute only.
A program may use at most 128 MiB of HBM per device.

```python
import jax
import jax.numpy as jnp
from jax import lax

HEADS = 16
HEAD_DIM = 128
TOKENS = 4096
BRANCHES = 4
ATT_WIDTH = 2048


def draw_ctrl_q(key, part):
    key = jax.random.fold_in(key, 1)
    drawn = jax.random.normal(key, (BRANCHES, TOKENS, ATT_WIDTH), jnp.float32)
    return drawn.astype(jnp.bfloat16)


def draw_ctrl_k(key, part):
    key = jax.random.fold_in(key, 2)
    drawn = jax.random.normal(key, (BRANCHES, TOKENS, ATT_WIDTH), jnp.float32)
    return drawn.astype(jnp.bfloat16)


def draw_base_q(key, part):
    key = jax.random.fold_in(key, 3)
    drawn = jax.random.normal(key, (TOKENS, ATT_WIDTH), jnp.float32)
    return drawn.astype(jnp.bfloat16)


def draw_base_k(key, part):
    key = jax.random.fold_in(key, 4)
    drawn = jax.random.normal(key, (TOKENS, ATT_WIDTH), jnp.float32)
    return drawn.astype(jnp.bfloat16)


def plant(values, stream_key, least, high):
    extent = values.shape
    index_at = [jax.random.randint(jax.random.fold_in(stream_key, axis), (), 0, extent[axis]) for axis in range(len(extent))]
    values = values.at[tuple(index_at)].set(least)
    longest = extent.index(max(extent))
    index_at[longest] = (index_at[longest] + 1) % extent[longest]
    return values.at[tuple(index_at)].set(high)


def level_of(stream_key, shape, shards, smallest, largest):
    def one(position, shards_of):
        heights = jax.random.uniform(jax.random.fold_in(jax.random.fold_in(stream_key, 6), position), (shards_of,), jnp.float32, smallest / len(shards), largest / len(shards))
        return jnp.repeat(jnp.exp(heights), shape[position] // shards_of).reshape((-1,) + (1,) * (len(shape) - position - 1))

    gain = one(*shards[0])
    for cut in shards[1:]:
        gain = gain * one(*cut)
    return gain


def bell_draw(rng, shape, width, limit, cuts=(), kind=jnp.bfloat16):
    factor_of = level_of(rng, shape, cuts, -0.22, 0.18) if cuts else 1.0
    drawn = jax.random.normal(rng, shape, jnp.float32) * width * factor_of
    return jnp.minimum(jnp.maximum(drawn, -limit), limit).astype(kind)


def setup_inputs(seed: int = 0) -> dict:
    key_of = jax.random.split(jax.random.key(seed), 8)
    return {
        "ctrl_q": draw_ctrl_q(jax.random.fold_in(key_of[7], 71), 0),
        "ctrl_k": draw_ctrl_k(jax.random.fold_in(key_of[7], 71), 0),
        "ctrl_v": bell_draw(key_of[2], (BRANCHES, TOKENS, ATT_WIDTH), 16.0, 96.0, ((0, 4), (1, 64))),
        "joining_codes": plant(jax.random.randint(key_of[3], (BRANCHES, TOKENS), 0, 33), jax.random.fold_in(key_of[3], 1), 0, 32).astype(jnp.int32),
        "base_q": draw_base_q(jax.random.fold_in(key_of[7], 71), 0),
        "base_k": draw_base_k(jax.random.fold_in(key_of[7], 71), 0),
        "base_v": bell_draw(key_of[6], (TOKENS, ATT_WIDTH), 8.0, 48.0, ((0, 64), (1, 4))),
    }


def attend_heads(queries, keys, values):
    tokens = queries.shape[0]

    def stack(matrix):
        return jnp.transpose(matrix.reshape(tokens, HEADS, HEAD_DIM), (1, 0, 2))

    def one_head(triple):
        query_rows, key_rows, value_rows = triple
        scores = jnp.dot(query_rows, key_rows.T, preferred_element_type=jnp.float32) * (HEAD_DIM ** -0.5)
        expo = jnp.exp(scores - jnp.max(scores, axis=1, keepdims=True))
        total = jnp.sum(expo, axis=1, keepdims=True)
        return jnp.dot(expo.astype(jnp.bfloat16), value_rows, preferred_element_type=jnp.float32) / total

    attended = lax.map(one_head, (stack(queries), stack(keys), stack(values)))
    return jnp.transpose(attended, (1, 0, 2)).reshape(tokens, HEADS * HEAD_DIM)


def branch_residual(triple):
    return attend_heads(triple[0], triple[1], triple[2])


def reference(ctrl_q, ctrl_k, ctrl_v, joining_codes, base_q, base_k, base_v):
    residual = lax.map(branch_residual, (ctrl_q, ctrl_k, ctrl_v))
    factors = joining_codes.astype(jnp.float32) / 16.0
    joined = jnp.sum(residual * factors[:, :, None], axis=0)
    base_values = (base_v.astype(jnp.float32) + joined).astype(jnp.bfloat16)
    base_out = attend_heads(base_q, base_k, base_values).astype(jnp.bfloat16)
    return (joined, base_out)
```

```python
import functools

import jax
import jax.numpy as jnp
from jax import lax
from jax.experimental import pallas as pl
from jax.experimental.pallas import tpu as pltpu
from jax.sharding import Mesh, PartitionSpec as P

HEADS = 16
DIM = 128
SCALE2 = DIM ** -0.5 * 1.4426950408889634
BF, F32 = jnp.bfloat16, jnp.float32
MIB = 1 << 20
VM = pl.BlockSpec(memory_space=pltpu.VMEM)
SM = pl.BlockSpec(memory_space=pltpu.SMEM)


def call(body, outs, operands, specs=None, vmem=16, flops=0, scratch=()):
    moved = sum(o.size * o.dtype.itemsize for o in [*operands, *outs])
    return pl.pallas_call(
        body,
        out_shape=outs,
        in_specs=specs or [VM] * len(operands),
        out_specs=[VM] * len(outs),
        scratch_shapes=list(scratch),
        compiler_params=pltpu.CompilerParams(vmem_limit_bytes=vmem * MIB),
        cost_estimate=pl.CostEstimate(flops=flops, bytes_accessed=moved, transcendentals=0),
    )(*operands)


def sds(shape, dtype=BF):
    return jax.ShapeDtypeStruct(shape, dtype)


def dot_nt(a, b):
    return lax.dot_general(a, b, (((1,), (1,)), ((), ())), preferred_element_type=F32)


def dot_nn(a, b):
    return lax.dot_general(a, b, (((1,), (0,)), ((), ())), preferred_element_type=F32)


def pack_kernel(k_ref, v_ref, q_ref, code_ref, out_ref):
    row = code_ref[...].astype(F32)
    row = jnp.concatenate([row, jnp.zeros((1, 64), F32)], axis=1)
    rows = jnp.broadcast_to(row, (16, 128)).astype(BF)
    for h in range(HEADS):
        cols = slice(h * DIM, (h + 1) * DIM)
        out_ref[h, 0:64] = k_ref[:, cols]
        out_ref[h, 64:128] = v_ref[:, cols]
        out_ref[h, 128:192] = q_ref[:, cols]
        out_ref[h, 192:208] = rows


def unpack_kernel(in_ref, k_ref, v_ref, q_ref, factor_ref):
    lane = lax.broadcasted_iota(jnp.int32, (64, 128), 1)
    sub = lax.broadcasted_iota(jnp.int32, (64, 128), 0)
    for t in range(16):
        rows = slice(t * 64, (t + 1) * 64)
        k_ref[rows] = in_ref[t, 0:64]
        v_ref[rows] = in_ref[t, 64:128]
        q_ref[rows] = in_ref[t, 128:192]
        code = in_ref[t, 192:208].astype(F32)[0:1]
        code = jnp.broadcast_to(code, (64, 128))
        col = jnp.sum(jnp.where(lane == sub, code, 0.0), axis=1, keepdims=True)
        factor_ref[rows] = col / 16.0


def score_kernel(q_ref, k_ref, p_ref, m_ref, l_ref):
    for i in range(4):
        rows = slice(i * 256, (i + 1) * 256)
        s = dot_nt(q_ref[rows], k_ref[...])
        m = jnp.max(s, axis=1, keepdims=True)
        p = jnp.exp2((s - m) * SCALE2)
        m_ref[rows] = m
        l_ref[rows] = jnp.sum(p, axis=1, keepdims=True)
        p_ref[rows] = p.astype(BF)


def value_kernel(p_ref, v_ref, acc_ref):
    for i in range(4):
        rows = slice(i * 256, (i + 1) * 256)
        acc_ref[rows] = dot_nn(p_ref[rows], v_ref[...])


def finish_kernel(b_ref, factor_ref, *refs):
    ms, ls, (acc0, p1, v1, p2, v2, p3, v3), outs = refs[0:4], refs[4:8], refs[8:15], refs[15:]
    b = b_ref[0]
    for i in (3, 2, 1, 0):
        rows = pl.ds(pl.multiple_of((b ^ i) * 256, 256), 256)
        m = [r[rows] for r in ms]
        best = jnp.maximum(jnp.maximum(m[0], m[1]), jnp.maximum(m[2], m[3]))
        w = [jnp.exp2((x - best) * SCALE2) for x in m]
        total = sum(w[c] * ls[c][rows] for c in range(4))
        acc = acc0[rows] * w[0]
        for c, (p, v) in ((1, (p1, v1)), (3, (p3, v3)), (2, (p2, v2))):
            acc = acc + dot_nn(p[rows], v[...]) * w[c]
        acc = acc / total * factor_ref[rows]
        outs[i][...] = acc.astype(outs[i].dtype)


def base_score_kernel(at_ref, q_ref, k_ref, p_ref, l_ref):
    yl, co, x = at_ref[0], at_ref[1], at_ref[2]
    blocks = []
    for cr in range(2):
        for xr in range(4):
            for yr in range(2):
                first = ((yl ^ yr) * 2 + (co ^ cr)) * 4 + ((x + 4 - xr) & 3)
                keys = k_ref[pl.ds(pl.multiple_of(first * 256, 256), 256)]
                blocks.append(dot_nt(q_ref[...], keys))
    best = functools.reduce(jnp.maximum, blocks)
    best = jnp.max(best, axis=1, keepdims=True)
    total = None
    for n, s in enumerate(blocks):
        p = jnp.exp2((s - best) * SCALE2)
        p_ref[n // 2, :, (n % 2) * 256 : (n % 2 + 1) * 256] = p.astype(BF)
        total = p if total is None else total + p
    l_ref[...] = jnp.sum(total, axis=1, keepdims=True)


def base_value_kernel(p_ref, l_ref, joined_ref, *refs):
    acc = None
    for n, v in enumerate(refs[:-1]):
        part = dot_nn(p_ref[n], v[...])
        acc = part if acc is None else acc + part
    out = (acc / l_ref[...]).astype(BF)
    joined = joined_ref[...].astype(BF)
    for t in range(4):
        rows = slice(t * 64, (t + 1) * 64)
        refs[-1][t, 0:64] = joined[rows]
        refs[-1][t, 64:128] = out[rows]


def home_kernel(in_ref, joined_ref, out_ref):
    for i in range(4):
        cols = slice(i * DIM, (i + 1) * DIM)
        joined_ref[:, cols] = in_ref[i, 0:64].astype(F32)
        out_ref[:, cols] = in_ref[i, 64:128]


def base_pack_kernel(k_ref, v_ref, q_ref, out_ref):
    for i in range(4):
        cols = slice(i * DIM, (i + 1) * DIM)
        out_ref[i, 0:64] = k_ref[:, cols]
        out_ref[i, 64:128] = v_ref[:, cols]
        out_ref[i, 128:192] = q_ref[:, cols]


def swap(values):
    perm = [(b * 16 + c * 4 + z, c * 16 + b * 4 + z) for b in range(4) for c in range(4) for z in range(4)]
    return lax.ppermute(values, ("yl", "co", "yh", "zh", "zl"), perm)


def along_x(values, step):
    return lax.ppermute(values, "x", [(j, (j + step) % 4) for j in range(4)])


def other(values, axis):
    return lax.ppermute(values, axis, [(0, 1), (1, 0)])


def shards(ctrl_q, ctrl_k, ctrl_v, codes, base_q, base_k, base_v):
    at = jnp.stack([lax.axis_index("yl"), lax.axis_index("co"), lax.axis_index("x")]).astype(jnp.int32)
    branch = (at[0] * 2 + at[1]).reshape(1)

    (base,) = call(base_pack_kernel, [sds((4, 192, DIM))], [base_k, base_v, base_q])
    base = swap(lax.all_to_all(base, "zl", 0, 0, tiled=True))
    base_keys, base_vals, base_quer = (base[:, 64 * i : 64 * i + 64].reshape(256, DIM) for i in range(3))
    base_keys = lax.all_gather(base_keys, ("yl", "co", "x"), axis=0, tiled=True)

    (packed,) = call(pack_kernel, [sds((HEADS, 208, DIM))], [ctrl_k[0], ctrl_v[0], ctrl_q[0], codes])
    packed = lax.all_to_all(packed, ("yh", "zh", "zl"), 0, 0, tiled=True)
    own_k, own_v, quer, factor = call(
        unpack_kernel, [sds((1024, DIM))] * 3 + [sds((1024, 1), F32)], [packed]
    )
    keys, vals = [own_k] + [None] * 3, [own_v] + [None] * 3
    for step in (1, 3, 2):
        keys[step] = along_x(own_k, step)
    for step in (1, 3, 2):
        vals[step] = along_x(own_v, step)
    scored = [
        call(
            score_kernel,
            [sds((1024, 1024)), sds((1024, 1), F32), sds((1024, 1), F32)],
            [quer, k],
            vmem=24,
            flops=2 * 1024 * 1024 * 128,
        )
        for k in keys
    ]
    ps, ms, ls = zip(*scored)
    (acc0,) = call(value_kernel, [sds((1024, DIM), F32)], [ps[0], vals[0]], flops=2 * 1024 * 1024 * 128)
    operands = [branch, factor, *ms, *ls, acc0, ps[1], vals[1], ps[2], vals[2], ps[3], vals[3]]
    outs = call(
        finish_kernel,
        [sds((256, DIM), F32)] + [sds((256, DIM))] * 3,
        operands,
        specs=[SM] + [VM] * (len(operands) - 1),
        vmem=28,
        flops=3 * 2 * 1024 * 1024 * 128,
    )

    joined = outs[0]
    for k in (3, 2, 1):
        joined = joined + lax.ppermute(outs[k], ("yl", "co"), [(j, j ^ k) for j in range(4)]).astype(F32)
    base_values = (base_vals.astype(F32) + joined).astype(BF)

    base_p, base_l = call(
        base_score_kernel,
        [sds((8, 256, 512)), sds((256, 1), F32)],
        [at, base_quer, base_keys],
        specs=[SM, VM, VM],
        vmem=24,
        flops=2 * 256 * 4096 * 128,
    )
    pair = jnp.concatenate([base_values, other(base_values, "yl")], axis=0)
    mine = [pair] + [None] * 3
    for step in (1, 3, 2):
        mine[step] = along_x(pair, step)
    theirs = [other(v, "co") for v in mine]
    (result,) = call(
        base_value_kernel, [sds((4, 128, DIM))], [base_p, base_l, joined, *mine, *theirs], flops=2 * 256 * 4096 * 128
    )
    result = lax.all_to_all(swap(result), "zl", 0, 0, tiled=True)
    return call(home_kernel, [sds((64, 512), F32), sds((64, 512))], [result])


def solution(mesh):
    fine = Mesh(mesh.devices.reshape(2, 2, 4, 2, 2, 4), ("yl", "co", "x", "yh", "zh", "zl"))
    branch, seq = ("yl", "co"), ("x", "yh", "zh", "zl")
    return jax.shard_map(
        shards,
        mesh=fine,
        in_specs=(P(branch, seq, None),) * 3 + (P(branch, seq),) + (P(seq, branch),) * 3,
        out_specs=(P(seq, branch), P(seq, branch)),
        check_vma=False,
    )
```

```python
import functools

import jax
import jax.numpy as jnp
from jax import lax
from jax.experimental import pallas as pl
from jax.experimental.pallas import tpu as pltpu
from jax.sharding import Mesh, PartitionSpec as P

HEADS = 16
DIM = 128
SCALE2 = DIM ** -0.5 * 1.4426950408889634
BF, F32 = jnp.bfloat16, jnp.float32
MIB = 1 << 20
VM = pl.BlockSpec(memory_space=pltpu.VMEM)
SM = pl.BlockSpec(memory_space=pltpu.SMEM)
ANY = pl.BlockSpec(memory_space=pltpu.HBM)


def call(body, outs, operands, specs=None, out_specs=None, vmem=16, flops=0, scratch=()):
    moved = sum(o.size * o.dtype.itemsize for o in [*operands, *outs])
    return pl.pallas_call(
        body,
        out_shape=outs,
        in_specs=specs or [VM] * len(operands),
        out_specs=out_specs or [VM] * len(outs),
        scratch_shapes=list(scratch),
        compiler_params=pltpu.CompilerParams(vmem_limit_bytes=vmem * MIB),
        cost_estimate=pl.CostEstimate(flops=flops, bytes_accessed=moved, transcendentals=0),
    )(*operands)


def sds(shape, dtype=BF):
    return jax.ShapeDtypeStruct(shape, dtype)


def dot_nt(a, b):
    return lax.dot_general(a, b, (((1,), (1,)), ((), ())), preferred_element_type=F32)


def dot_nn(a, b):
    return lax.dot_general(a, b, (((1,), (0,)), ((), ())), preferred_element_type=F32)


def pack_kernel(k_ref, v_ref, q_ref, code_ref, out_ref, code_row, held, sem):
    code = pltpu.make_async_copy(code_ref, code_row, sem.at[48])
    code.start()
    copies = []
    for place in range(HEADS):
        yh, zt, zp = place // 8, place // 2 % 4, place % 2
        head = (yh * 2 + zp) * 4 + zt
        for n, ref in enumerate((k_ref, v_ref, q_ref)):
            source = ref.at[0, :, pl.ds(head * DIM, DIM)]
            target = held.at[place, pl.ds(n * 64, 64)]
            copies.append(pltpu.make_async_copy(source, target, sem.at[place * 3 + n]))
    for copy in copies:
        copy.start()
    code.wait()
    row = jnp.concatenate([code_row[...].astype(F32), jnp.zeros((1, 64), F32)], axis=1)
    held[:, 192:208] = jnp.broadcast_to(row.reshape(1, 1, 128), (HEADS, 16, DIM)).astype(BF)
    for copy in copies:
        copy.wait()
    last = pltpu.make_async_copy(held, out_ref, sem.at[49])
    last.start()
    last.wait()


def base_pack_kernel(at_ref, k_ref, v_ref, q_ref, *refs):
    outs, sem = refs[:4], refs[4]
    copies = []
    for step, out in enumerate(outs):
        head = (at_ref[3] + step) & 3
        for n, ref in enumerate((k_ref, v_ref, q_ref)):
            source = ref.at[:, pl.ds(pl.multiple_of(head * DIM, DIM), DIM)]
            target = out.at[pl.ds(n * 64, 64)]
            copies.append(pltpu.make_async_copy(source, target, sem.at[step * 3 + n]))
    for copy in copies:
        copy.start()
    for copy in copies:
        copy.wait()


def base_unpack_kernel(at_ref, *refs):
    ins, (kv_ref, q_ref) = refs[:4], refs[4:]
    for step, ref in enumerate(ins):
        first = ((at_ref[3] + 4 - step) & 3) * 64
        kv_ref[pl.ds(pl.multiple_of(first, 64), 64)] = ref[0:64]
        kv_ref[pl.ds(pl.multiple_of(256 + first, 64), 64)] = ref[64:128]
        q_ref[pl.ds(pl.multiple_of(first, 64), 64)] = ref[128:192]


def unpack_kernel(in_ref, after_ref, kv_ref, q_ref, factor_ref):
    del after_ref
    lane = lax.broadcasted_iota(jnp.int32, (64, 128), 1)
    sub = lax.broadcasted_iota(jnp.int32, (64, 128), 0)
    for place in range(16):
        yh, zt, zp = place // 8, place // 2 % 4, place % 2
        t = (yh * 2 + zp) * 4 + zt
        rows = slice(t * 64, (t + 1) * 64)
        first = t // 8 * 1024 + t % 8 * 64
        kv_ref[first : first + 64] = in_ref[place, 0:64]
        kv_ref[first + 512 : first + 576] = in_ref[place, 64:128]
        q_ref[rows] = in_ref[place, 128:192]
        code = in_ref[place, 192:208].astype(F32)[0:1]
        code = jnp.broadcast_to(code, (64, 128))
        col = jnp.sum(jnp.where(lane == sub, code, 0.0), axis=1, keepdims=True)
        factor_ref[rows] = col / 16.0


def score_kernel(q_ref, *refs):
    halves, (p_ref, m_ref, l_ref) = refs[:-3], refs[-3:]
    keys = [halves[0], halves[-1]]
    starts = (0, 0 if len(halves) == 2 else 1024)
    for i in range(4):
        rows = slice(i * 256, (i + 1) * 256)
        s = jnp.concatenate([dot_nt(q_ref[rows], k[a : a + 512]) for k, a in zip(keys, starts)], axis=1)
        m = jnp.max(s, axis=1, keepdims=True)
        p = jnp.exp2((s - m) * SCALE2)
        m_ref[rows] = m
        l_ref[rows] = jnp.sum(p, axis=1, keepdims=True)
        p_ref[rows] = p.astype(BF)


def merge(rows, ms, ls):
    m = [r[rows] for r in ms]
    best = functools.reduce(jnp.maximum, m)
    weights = [jnp.exp2((x - best) * SCALE2) for x in m]
    return best, weights, sum(w * l[rows] for w, l in zip(weights, ls))


def middle_kernel(*refs):
    ms, ls, ps, vs, (m_ref, l_ref, acc_ref) = refs[0:3], refs[3:6], refs[6:9], refs[9:12], refs[12:]
    for i in range(4):
        rows = slice(i * 256, (i + 1) * 256)
        best, weights, total = merge(rows, ms, ls)
        m_ref[rows] = best
        l_ref[rows] = total
        acc_ref[rows] = sum(
            (dot_nn(p[rows, 0:512], v[512:1024]) + dot_nn(p[rows, 512:1024], v[1536:2048])) * w
            for p, v, w in zip(ps, vs, weights)
        )


def finish_kernel(at_ref, factor_ref, *refs):
    ms, ls, acc_ref, p_ref, va_ref, vb_ref, keep_ref, give_ref = refs[0:2], refs[2:4], *refs[4:]
    b = at_ref[0] * 2 + at_ref[1]
    for chunk, out, place in ((1, give_ref, 0), (3, give_ref, 1), (0, keep_ref, 0), (2, keep_ref, 1)):
        rows = pl.ds(pl.multiple_of((b ^ chunk) * 256, 256), 256)
        _, weights, total = merge(rows, ms, ls)
        far = dot_nn(p_ref[rows, 0:512], va_ref[512:1024]) + dot_nn(p_ref[rows, 512:1024], vb_ref[512:1024])
        acc = acc_ref[rows] * weights[0] + far * weights[1]
        acc = acc / total * factor_ref[rows]
        out[place * 256 : place * 256 + 256] = acc.astype(out.dtype)


def pair_kernel(keep_ref, got_ref, pair_ref, send_ref):
    pair = keep_ref[...] + got_ref[...].astype(F32)
    pair_ref[...] = pair
    send_ref[...] = pair.astype(BF)


def join_kernel(pair_ref, got_ref, bv_ref, more_ref, after_ref, joined_ref, values_ref):
    del after_ref
    for n, base in enumerate((bv_ref, more_ref)):
        rows = slice(n * 256, n * 256 + 256)
        joined = pair_ref[rows] + got_ref[256 - n * 256 : 512 - n * 256].astype(F32)
        if n == 0:
            joined_ref[...] = joined.astype(BF)
        values_ref[rows] = (base[256:512].astype(F32) + joined).astype(BF)


def base_pair_kernel(kv_ref, more_ref, out_ref):
    out_ref[0:256] = kv_ref[0:256]
    out_ref[256:512] = more_ref[0:256]


def base_score_kernel(q_ref, *refs):
    keys, (p_ref, l_ref) = refs[:8], refs[8:]
    blocks = [dot_nt(q_ref[...], k[...]) for k in keys]
    best = jnp.max(functools.reduce(jnp.maximum, blocks), axis=1, keepdims=True)
    total = None
    for n, s in enumerate(blocks):
        p = jnp.exp2((s - best) * SCALE2)
        p_ref[n] = p.astype(BF)
        total = p if total is None else total + p
    l_ref[...] = jnp.sum(total, axis=1, keepdims=True)


def base_value_kernel(at_ref, p_ref, l_ref, joined_ref, *refs):
    values, outs, held = refs[:8], refs[8:12], refs[12]
    acc = None
    for n, v in enumerate(values):
        part = dot_nn(p_ref[n], v[...])
        acc = part if acc is None else acc + part
    held[...] = (acc / l_ref[...]).astype(BF)
    for step, out in enumerate(outs):
        rows = pl.ds(pl.multiple_of(((at_ref[3] + step) & 3) * 64, 64), 64)
        out[0:64] = joined_ref[rows]
        out[64:128] = held[rows]


def home_kernel(at_ref, in_ref, joined_ref, out_ref):
    for step in range(4):
        head = (at_ref[3] + 4 - step) & 3
        cols = pl.ds(pl.multiple_of(head * DIM, DIM), DIM)
        joined_ref[:, cols] = in_ref[step, 0:64].astype(F32)
        out_ref[:, cols] = in_ref[step, 64:128]


def swap(values, step=0):
    def place(b, c, z):
        return ((b * 2 + c // 2) * 4 + z) * 2 + c % 2

    perm = [
        (place(b, c, z), place(c, b, (z + step) % 4)) for b in range(4) for c in range(4) for z in range(4)
    ]
    return lax.ppermute(values, ("yl", "co", "yh", "zt", "zp"), perm)


def along(axis, values, step):
    return lax.ppermute(values, axis, [(j, (j + step) % 4) for j in range(4)])


def other(values, axis):
    return lax.ppermute(values, axis, [(0, 1), (1, 0)])


def gather_pair(pair):
    mine = [pair] + [None] * 3
    for step in (1, 3, 2):
        mine[step] = along("x", pair, step)
    return mine + [other(v, "co") for v in mine]


def shards(ctrl_q, ctrl_k, ctrl_v, codes, base_q, base_k, base_v):
    at = jnp.stack([lax.axis_index(a) for a in ("yl", "co", "x", "zt")]).astype(jnp.int32)

    (packed,) = call(
        pack_kernel,
        [sds((HEADS, 208, DIM))],
        [ctrl_k, ctrl_v, ctrl_q, codes],
        specs=[ANY] * 4,
        out_specs=[ANY],
        vmem=60,
        scratch=[pltpu.VMEM((1, 64), jnp.int32), pltpu.VMEM((HEADS, 208, DIM), BF), pltpu.SemaphoreType.DMA((50,))],
    )
    sent = lax.all_to_all(packed, ("yh", "zt", "zp"), 0, 0, tiled=True)

    parts = call(
        base_pack_kernel,
        [sds((192, DIM))] * 4,
        [at, base_k, base_v, base_q],
        specs=[SM] + [ANY] * 3,
        out_specs=[ANY] * 4,
        scratch=[pltpu.SemaphoreType.DMA((12,))],
    )
    parts = [swap(part, step) for step, part in enumerate(parts)]
    base_kv, base_quer = call(
        base_unpack_kernel, [sds((512, DIM)), sds((256, DIM))], [at, *parts], specs=[SM] + [VM] * 4
    )
    own, quer, factor = call(
        unpack_kernel, [sds((2048, DIM)), sds((1024, DIM)), sds((1024, 1), F32)], [sent, base_quer], specs=[VM, pl.BlockSpec(memory_space=pl.ANY)]
    )
    after, before = along("x", own, 1), along("x", own, 3)
    far = [along("x", after[:1024], 1), along("x", before[1024:], 3)]

    more_kv = other(base_kv, "yl")
    (base_pair,) = call(
        base_pair_kernel,
        [sds((512, DIM))],
        [base_kv, more_kv],
    )
    base_keys = gather_pair(base_pair)
    base_p, base_l = call(
        base_score_kernel,
        [sds((8, 256, 512)), sds((256, 1), F32)],
        [base_quer, *base_keys],
        vmem=24,
        flops=2 * 256 * 4096 * 128,
    )

    outs = [sds((1024, 1024)), sds((1024, 1), F32), sds((1024, 1), F32)]
    scored = [
        call(score_kernel, outs, [quer, kv], vmem=24, flops=2 * 1024 * 1024 * 128) for kv in (own, after, before)
    ]
    ps, ms, ls = zip(*scored)
    m, l, acc = call(
        middle_kernel,
        [sds((1024, 1), F32), sds((1024, 1), F32), sds((1024, DIM), F32)],
        [*ms, *ls, *ps, own, after, before],
        vmem=24,
        flops=3 * 2 * 1024 * 1024 * 128,
    )
    far_p, far_m, far_l = call(score_kernel, outs, [quer, *far], vmem=24, flops=2 * 1024 * 1024 * 128)
    keep, give = call(
        finish_kernel,
        [sds((512, DIM), F32), sds((512, DIM))],
        [at, factor, m, far_m, l, far_l, acc, far_p, *far],
        specs=[SM] + [VM] * 9,
        vmem=24,
        flops=2 * 1024 * 1024 * 128,
    )

    pair, send = call(pair_kernel, [sds((512, DIM), F32), sds((512, DIM))], [keep, other(give, "co")])
    joined, base_values = call(
        join_kernel, [sds((256, DIM)), sds((512, DIM))], [pair, other(send, "yl"), base_kv, more_kv, base_l], specs=[VM] * 4 + [pl.BlockSpec(memory_space=pl.ANY)]
    )

    outs = call(
        base_value_kernel,
        [sds((128, DIM))] * 4,
        [at, base_p, base_l, joined, *gather_pair(base_values)],
        specs=[SM] + [VM] * 11,
        flops=2 * 256 * 4096 * 128,
        scratch=[pltpu.VMEM((256, DIM), BF)],
    )
    result = [outs[0]] + [None] * 3
    for step in (1, 3, 2):
        result[step] = along("zt", outs[step], step)
    result = swap(jnp.stack(result))
    return call(home_kernel, [sds((64, 512), F32), sds((64, 512))], [at, result], specs=[SM, VM])


def solution(mesh):
    fine = Mesh(mesh.devices.reshape(2, 2, 4, 2, 4, 2), ("yl", "co", "x", "yh", "zt", "zp"))
    branch, seq = ("yl", "co"), ("x", "yh", "zt", "zp")
    return jax.shard_map(
        shards,
        mesh=fine,
        in_specs=(P(branch, seq, None),) * 3 + (P(branch, seq),) + (P(seq, branch),) * 3,
        out_specs=(P(seq, branch), P(seq, branch)),
        check_vma=False,
    )
```

```python
import functools

import jax
import jax.numpy as jnp
from jax import lax
from jax.experimental import pallas as pl
from jax.experimental.pallas import tpu as pltpu
from jax.sharding import Mesh, PartitionSpec as P

HEADS = 16
DIM = 128
SCALE2 = DIM ** -0.5 * 1.4426950408889634
BF, F32 = jnp.bfloat16, jnp.float32
MIB = 1 << 20
VM = pl.BlockSpec(memory_space=pltpu.VMEM)
SM = pl.BlockSpec(memory_space=pltpu.SMEM)
ANY = pl.BlockSpec(memory_space=pltpu.HBM)
ANYWHERE = pl.BlockSpec(memory_space=pl.ANY)


def call(body, outs, operands, specs=None, out_specs=None, vmem=16, flops=0, scratch=(), aliases={}):
    moved = sum(o.size * o.dtype.itemsize for o in [*operands, *outs])
    return pl.pallas_call(
        body,
        out_shape=outs,
        in_specs=specs or [VM] * len(operands),
        out_specs=out_specs or [VM] * len(outs),
        scratch_shapes=list(scratch),
        input_output_aliases=aliases,
        compiler_params=pltpu.CompilerParams(vmem_limit_bytes=vmem * MIB),
        cost_estimate=pl.CostEstimate(flops=flops, bytes_accessed=moved, transcendentals=0),
    )(*operands)


def sds(shape, dtype=BF):
    return jax.ShapeDtypeStruct(shape, dtype)


def dot_nt(a, b):
    return lax.dot_general(a, b, (((1,), (1,)), ((), ())), preferred_element_type=F32)


def dot_nn(a, b):
    return lax.dot_general(a, b, (((1,), (0,)), ((), ())), preferred_element_type=F32)


def pack_kernel(k_ref, v_ref, q_ref, code_ref, out_ref, code_row, held, sem):
    code = pltpu.make_async_copy(code_ref, code_row, sem.at[48])
    code.start()
    copies = []
    for place in range(HEADS):
        yh, zt, zp = place // 8, place // 2 % 4, place % 2
        head = (yh * 2 + zp) * 4 + zt
        for n, ref in enumerate((k_ref, v_ref, q_ref)):
            source = ref.at[0, :, pl.ds(head * DIM, DIM)]
            target = held.at[place, pl.ds(n * 64, 64)]
            copies.append(pltpu.make_async_copy(source, target, sem.at[place * 3 + n]))
    for copy in copies:
        copy.start()
    code.wait()
    row = jnp.concatenate([code_row[...].astype(F32), jnp.zeros((1, 64), F32)], axis=1)
    held[:, 192:208] = jnp.broadcast_to(row.reshape(1, 1, 128), (HEADS, 16, DIM)).astype(BF)
    for copy in copies:
        copy.wait()
    last = pltpu.make_async_copy(held, out_ref, sem.at[49])
    last.start()
    last.wait()


def base_pack_kernel(at_ref, k_ref, v_ref, q_ref, *refs):
    outs, sem = refs[:4], refs[4]
    copies = []
    for step, out in enumerate(outs):
        head = (at_ref[3] + step) & 3
        for n, ref in enumerate((k_ref, v_ref, q_ref)):
            source = ref.at[:, pl.ds(pl.multiple_of(head * DIM, DIM), DIM)]
            target = out.at[pl.ds(n * 64, 64)]
            copies.append(pltpu.make_async_copy(source, target, sem.at[step * 3 + n]))
    for copy in copies:
        copy.start()
    for copy in copies:
        copy.wait()


def base_unpack_kernel(at_ref, *refs):
    ins, (kv_ref, q_ref) = refs[:4], refs[4:]
    for step, ref in enumerate(ins):
        first = ((at_ref[3] + 4 - step) & 3) * 64
        kv_ref[pl.ds(pl.multiple_of(first, 64), 64)] = ref[0:64]
        kv_ref[pl.ds(pl.multiple_of(256 + first, 64), 64)] = ref[64:128]
        q_ref[pl.ds(pl.multiple_of(first, 64), 64)] = ref[128:192]


def unpack_kernel(in_ref, after_ref, k_ref, v_ref, q_ref, factor_ref):
    del after_ref
    lane = lax.broadcasted_iota(jnp.int32, (64, 128), 1)
    sub = lax.broadcasted_iota(jnp.int32, (64, 128), 0)
    for place in range(16):
        yh, zt, zp = place // 8, place // 2 % 4, place % 2
        t = (yh * 2 + zp) * 4 + zt
        rows = slice(t * 64, (t + 1) * 64)
        k_ref[rows] = in_ref[place, 0:64]
        v_ref[rows] = in_ref[place, 64:128]
        q_ref[rows] = in_ref[place, 128:192]
        code = in_ref[place, 192:208].astype(F32)[0:1]
        code = jnp.broadcast_to(code, (64, 128))
        col = jnp.sum(jnp.where(lane == sub, code, 0.0), axis=1, keepdims=True)
        factor_ref[rows] = col / 16.0


def score_kernel(q_ref, *refs):
    keys, (p_ref, m_ref, l_ref) = refs[:-3], refs[-3:]
    for i in range(4):
        rows = slice(i * 256, (i + 1) * 256)
        parts = [dot_nt(q_ref[rows], k[...]) for k in keys]
        s = jnp.concatenate(parts, axis=1) if len(parts) > 1 else parts[0]
        m = jnp.max(s, axis=1, keepdims=True)
        p = jnp.exp2((s - m) * SCALE2)
        m_ref[rows] = m
        l_ref[rows] = jnp.sum(p, axis=1, keepdims=True)
        p_ref[rows] = p.astype(BF)


def own_score_kernel(q_ref, k_ref, v_ref, p_ref, m_ref, l_ref, same_v_ref):
    del v_ref, same_v_ref
    score_kernel(q_ref, k_ref, p_ref, m_ref, l_ref)


def merge(rows, ms, ls):
    m = [r[rows] for r in ms]
    best = functools.reduce(jnp.maximum, m)
    weights = [jnp.exp2((x - best) * SCALE2) for x in m]
    return best, weights, sum(w * l[rows] for w, l in zip(weights, ls))


def middle_kernel(*refs):
    ms, ls, ps, vs, (m_ref, l_ref, acc_ref) = refs[0:3], refs[3:6], refs[6:9], refs[9:12], refs[12:]
    for i in range(4):
        rows = slice(i * 256, (i + 1) * 256)
        best, weights, total = merge(rows, ms, ls)
        m_ref[rows] = best
        l_ref[rows] = total
        acc_ref[rows] = sum(dot_nn(p[rows], v[...]) * w for p, v, w in zip(ps, vs, weights))


def finish_kernel(at_ref, factor_ref, *refs):
    ms, ls, acc_ref, p_ref, va_ref, vb_ref, keep_ref, give_ref = refs[0:2], refs[2:4], *refs[4:]
    b = at_ref[0] * 2 + at_ref[1]
    for chunk, out, place in ((1, give_ref, 0), (3, give_ref, 1), (0, keep_ref, 0), (2, keep_ref, 1)):
        rows = pl.ds(pl.multiple_of((b ^ chunk) * 256, 256), 256)
        _, weights, total = merge(rows, ms, ls)
        far = dot_nn(p_ref[rows, 0:512], va_ref[...]) + dot_nn(p_ref[rows, 512:1024], vb_ref[...])
        acc = acc_ref[rows] * weights[0] + far * weights[1]
        acc = acc / total * factor_ref[rows]
        out[place * 256 : place * 256 + 256] = acc.astype(out.dtype)


def pair_kernel(keep_ref, got_ref, pair_ref, send_ref):
    pair = keep_ref[...] + got_ref[...].astype(F32)
    pair_ref[...] = pair
    send_ref[...] = pair.astype(BF)


def join_kernel(pair_ref, got_ref, bv_ref, more_ref, after_ref, joined_ref, values_ref):
    del after_ref
    for n, base in enumerate((bv_ref, more_ref)):
        rows = slice(n * 256, n * 256 + 256)
        joined = pair_ref[rows] + got_ref[256 - n * 256 : 512 - n * 256].astype(F32)
        if n == 0:
            joined_ref[...] = joined.astype(BF)
        values_ref[rows] = (base[256:512].astype(F32) + joined).astype(BF)


def base_pair_kernel(kv_ref, more_ref, out_ref):
    out_ref[0:256] = kv_ref[0:256]
    out_ref[256:512] = more_ref[0:256]


def base_score_kernel(q_ref, *refs):
    keys, (p_ref, l_ref) = refs[:8], refs[8:]
    blocks = [dot_nt(q_ref[...], k[...]) for k in keys]
    best = jnp.max(functools.reduce(jnp.maximum, blocks), axis=1, keepdims=True)
    total = None
    for n, s in enumerate(blocks):
        p = jnp.exp2((s - best) * SCALE2)
        p_ref[n] = p.astype(BF)
        total = p if total is None else total + p
    l_ref[...] = jnp.sum(total, axis=1, keepdims=True)


def base_value_kernel(at_ref, p_ref, l_ref, joined_ref, *refs):
    values, outs, held = refs[:8], refs[8:12], refs[12]
    acc = None
    for n, v in enumerate(values):
        part = dot_nn(p_ref[n], v[...])
        acc = part if acc is None else acc + part
    held[...] = (acc / l_ref[...]).astype(BF)
    for step, out in enumerate(outs):
        rows = pl.ds(pl.multiple_of(((at_ref[3] + step) & 3) * 64, 64), 64)
        out[0:64] = joined_ref[rows]
        out[64:128] = held[rows]


def home_kernel(at_ref, *refs):
    joined_ref, out_ref = refs[4:]
    for step in range(4):
        head = (at_ref[3] + 4 - step) & 3
        cols = pl.ds(pl.multiple_of(head * DIM, DIM), DIM)
        joined_ref[:, cols] = refs[step][0:64].astype(F32)
        out_ref[:, cols] = refs[step][64:128]


def swap(values, step=0):
    def place(b, c, z):
        return ((b * 2 + c // 2) * 4 + z) * 2 + c % 2

    perm = [
        (place(b, c, z), place(c, b, (z + step) % 4)) for b in range(4) for c in range(4) for z in range(4)
    ]
    return lax.ppermute(values, ("yl", "co", "yh", "zt", "zp"), perm)


def along(axis, values, step):
    return lax.ppermute(values, axis, [(j, (j + step) % 4) for j in range(4)])


def other(values, axis):
    return lax.ppermute(values, axis, [(0, 1), (1, 0)])


def gather_pair(pair):
    mine = [pair] + [None] * 3
    for step in (1, 3, 2):
        mine[step] = along("x", pair, step)
    return mine + [other(v, "co") for v in mine]


def shards(ctrl_q, ctrl_k, ctrl_v, codes, base_q, base_k, base_v):
    at = jnp.stack([lax.axis_index(a) for a in ("yl", "co", "x", "zt")]).astype(jnp.int32)

    (packed,) = call(
        pack_kernel,
        [sds((HEADS, 208, DIM))],
        [ctrl_k, ctrl_v, ctrl_q, codes],
        specs=[ANY] * 4,
        out_specs=[ANY],
        vmem=60,
        scratch=[pltpu.VMEM((1, 64), jnp.int32), pltpu.VMEM((HEADS, 208, DIM), BF), pltpu.SemaphoreType.DMA((50,))],
    )
    sent = lax.all_to_all(packed, ("yh", "zt", "zp"), 0, 0, tiled=True)

    parts = call(
        base_pack_kernel,
        [sds((192, DIM))] * 4,
        [at, base_k, base_v, base_q],
        specs=[SM] + [ANY] * 3,
        out_specs=[ANY] * 4,
        scratch=[pltpu.SemaphoreType.DMA((12,))],
    )
    parts = [swap(part, step) for step, part in enumerate(parts)]
    base_kv, base_quer = call(
        base_unpack_kernel, [sds((512, DIM)), sds((256, DIM))], [at, *parts], specs=[SM] + [VM] * 4
    )
    own_k, own_v, quer, factor = call(
        unpack_kernel,
        [sds((1024, DIM))] * 3 + [sds((1024, 1), F32)],
        [sent, base_quer],
        specs=[VM, ANYWHERE],
    )
    outs = [sds((1024, 1024)), sds((1024, 1), F32), sds((1024, 1), F32)]
    after_k, before_k = along("x", own_k, 1), along("x", own_k, 3)
    *own_score, own_v = call(
        own_score_kernel,
        outs + [sds((1024, DIM))],
        [quer, own_k, own_v],
        specs=[VM, VM, ANYWHERE],
        out_specs=[VM] * 3 + [ANYWHERE],
        vmem=24,
        flops=2 * 1024 * 1024 * 128,
        aliases={2: 3},
    )
    after_v, before_v = along("x", own_v, 1), along("x", own_v, 3)
    far_k = [along("x", after_k[:512], 1), along("x", before_k[512:], 3)]
    far_v = [along("x", after_v[:512], 1), along("x", before_v[512:], 3)]

    more_kv = other(base_kv, "yl")
    (base_pair,) = call(
        base_pair_kernel,
        [sds((512, DIM))],
        [base_kv, more_kv],
    )
    base_keys = gather_pair(base_pair)
    base_p, base_l = call(
        base_score_kernel,
        [sds((8, 256, 512)), sds((256, 1), F32)],
        [base_quer, *base_keys],
        vmem=24,
        flops=2 * 256 * 4096 * 128,
    )

    scored = [own_score] + [
        call(score_kernel, outs, [quer, k], vmem=24, flops=2 * 1024 * 1024 * 128) for k in (after_k, before_k)
    ]
    ps, ms, ls = zip(*scored)
    m, l, acc = call(
        middle_kernel,
        [sds((1024, 1), F32), sds((1024, 1), F32), sds((1024, DIM), F32)],
        [*ms, *ls, *ps, own_v, after_v, before_v],
        vmem=24,
        flops=3 * 2 * 1024 * 1024 * 128,
    )
    far_p, far_m, far_l = call(score_kernel, outs, [quer, *far_k], vmem=24, flops=2 * 1024 * 1024 * 128)
    keep, give = call(
        finish_kernel,
        [sds((512, DIM), F32), sds((512, DIM))],
        [at, factor, m, far_m, l, far_l, acc, far_p, *far_v],
        specs=[SM] + [VM] * 9,
        vmem=24,
        flops=2 * 1024 * 1024 * 128,
    )

    pair, send = call(pair_kernel, [sds((512, DIM), F32), sds((512, DIM))], [keep, other(give, "co")])
    joined, base_values = call(
        join_kernel, [sds((256, DIM)), sds((512, DIM))], [pair, other(send, "yl"), base_kv, more_kv, base_l], specs=[VM] * 4 + [ANYWHERE]
    )

    outs = call(
        base_value_kernel,
        [sds((128, DIM))] * 4,
        [at, base_p, base_l, joined, *gather_pair(base_values)],
        specs=[SM] + [VM] * 11,
        flops=2 * 256 * 4096 * 128,
        scratch=[pltpu.VMEM((256, DIM), BF)],
    )
    result = [None] * 4
    for step in (0, 1, 3, 2):
        result[step] = swap(outs[step], step)
    return call(home_kernel, [sds((64, 512), F32), sds((64, 512))], [at, *result], specs=[SM] + [VM] * 4)


def solution(mesh):
    fine = Mesh(mesh.devices.reshape(2, 2, 4, 2, 4, 2), ("yl", "co", "x", "yh", "zt", "zp"))
    branch, seq = ("yl", "co"), ("x", "yh", "zt", "zp")
    return jax.shard_map(
        shards,
        mesh=fine,
        in_specs=(P(branch, seq, None),) * 3 + (P(branch, seq),) + (P(seq, branch),) * 3,
        out_specs=(P(seq, branch), P(seq, branch)),
        check_vma=False,
    )
```

```python
import functools

import jax
import jax.numpy as jnp
from jax import lax
from jax.experimental import pallas as pl
from jax.experimental.pallas import tpu as pltpu
from jax.sharding import Mesh, PartitionSpec as P

HEADS = 16
DIM = 128
SCALE2 = DIM ** -0.5 * 1.4426950408889634
BF, F32 = jnp.bfloat16, jnp.float32
MIB = 1 << 20
VM = pl.BlockSpec(memory_space=pltpu.VMEM)
SM = pl.BlockSpec(memory_space=pltpu.SMEM)
ANY = pl.BlockSpec(memory_space=pltpu.HBM)
ANYWHERE = pl.BlockSpec(memory_space=pl.ANY)


def call(body, outs, operands, specs=None, out_specs=None, vmem=16, flops=0, scratch=(), aliases={}):
    moved = sum(o.size * o.dtype.itemsize for o in [*operands, *outs])
    return pl.pallas_call(
        body,
        out_shape=outs,
        in_specs=specs or [VM] * len(operands),
        out_specs=out_specs or [VM] * len(outs),
        scratch_shapes=list(scratch),
        input_output_aliases=aliases,
        compiler_params=pltpu.CompilerParams(vmem_limit_bytes=vmem * MIB),
        cost_estimate=pl.CostEstimate(flops=flops, bytes_accessed=moved, transcendentals=0),
    )(*operands)


def sds(shape, dtype=BF):
    return jax.ShapeDtypeStruct(shape, dtype)


def dot_nt(a, b):
    return lax.dot_general(a, b, (((1,), (1,)), ((), ())), preferred_element_type=F32)


def dot_nn(a, b):
    return lax.dot_general(a, b, (((1,), (0,)), ((), ())), preferred_element_type=F32)


def pack_kernel(k_ref, v_ref, q_ref, code_ref, out_ref, code_row, held, sem):
    code = pltpu.make_async_copy(code_ref, code_row, sem.at[48])
    code.start()
    copies = []
    for place in range(HEADS):
        yh, zt, zp = place // 8, place // 2 % 4, place % 2
        head = (yh * 2 + zp) * 4 + zt
        for n, ref in enumerate((k_ref, v_ref, q_ref)):
            source = ref.at[0, :, pl.ds(head * DIM, DIM)]
            target = held.at[place, pl.ds(n * 64, 64)]
            copies.append(pltpu.make_async_copy(source, target, sem.at[place * 3 + n]))
    for copy in copies:
        copy.start()
    code.wait()
    row = jnp.concatenate([code_row[...].astype(F32), jnp.zeros((1, 64), F32)], axis=1)
    held[:, 192:208] = jnp.broadcast_to(row.reshape(1, 1, 128), (HEADS, 16, DIM)).astype(BF)
    for copy in copies:
        copy.wait()
    last = pltpu.make_async_copy(held, out_ref, sem.at[49])
    last.start()
    last.wait()


def base_pack_kernel(at_ref, k_ref, v_ref, q_ref, *refs):
    outs, sem = refs[:4], refs[4]
    copies = []
    for step, out in enumerate(outs):
        head = (at_ref[3] + step) & 3
        for n, ref in enumerate((k_ref, v_ref, q_ref)):
            source = ref.at[:, pl.ds(pl.multiple_of(head * DIM, DIM), DIM)]
            target = out.at[pl.ds(n * 64, 64)]
            copies.append(pltpu.make_async_copy(source, target, sem.at[step * 3 + n]))
    for copy in copies:
        copy.start()
    for copy in copies:
        copy.wait()


def base_unpack_kernel(at_ref, *refs):
    ins, (kv_ref, q_ref) = refs[:4], refs[4:]
    for step, ref in enumerate(ins):
        first = ((at_ref[3] + 4 - step) & 3) * 64
        kv_ref[pl.ds(pl.multiple_of(first, 64), 64)] = ref[0:64]
        kv_ref[pl.ds(pl.multiple_of(256 + first, 64), 64)] = ref[64:128]
        q_ref[pl.ds(pl.multiple_of(first, 64), 64)] = ref[128:192]


def unpack_kernel(in_ref, after_ref, k_ref, v_ref, q_ref, factor_ref):
    del after_ref
    lane = lax.broadcasted_iota(jnp.int32, (64, 128), 1)
    sub = lax.broadcasted_iota(jnp.int32, (64, 128), 0)
    for place in range(16):
        yh, zt, zp = place // 8, place // 2 % 4, place % 2
        t = (yh * 2 + zp) * 4 + zt
        rows = slice(t * 64, (t + 1) * 64)
        k_ref[rows] = in_ref[place, 0:64]
        v_ref[rows] = in_ref[place, 64:128]
        q_ref[rows] = in_ref[place, 128:192]
        code = in_ref[place, 192:208].astype(F32)[0:1]
        code = jnp.broadcast_to(code, (64, 128))
        col = jnp.sum(jnp.where(lane == sub, code, 0.0), axis=1, keepdims=True)
        factor_ref[rows] = col / 16.0


def score_kernel(q_ref, *refs):
    keys, (p_ref, m_ref, l_ref) = refs[:-3], refs[-3:]
    for i in range(4):
        rows = slice(i * 256, (i + 1) * 256)
        parts = [dot_nt(q_ref[rows], k[...]) for k in keys]
        s = jnp.concatenate(parts, axis=1) if len(parts) > 1 else parts[0]
        m = jnp.max(s, axis=1, keepdims=True)
        p = jnp.exp2((s - m) * SCALE2)
        m_ref[rows] = m
        l_ref[rows] = jnp.sum(p, axis=1, keepdims=True)
        p_ref[rows] = p.astype(BF)


def own_score_kernel(q_ref, k_ref, v_ref, p_ref, m_ref, l_ref, same_v_ref):
    del v_ref, same_v_ref
    score_kernel(q_ref, k_ref, p_ref, m_ref, l_ref)


def merge(rows, ms, ls):
    m = [r[rows] for r in ms]
    best = functools.reduce(jnp.maximum, m)
    weights = [jnp.exp2((x - best) * SCALE2) for x in m]
    return best, weights, sum(w * l[rows] for w, l in zip(weights, ls))


def middle_kernel(*refs):
    ms, ls, ps, vs, (m_ref, l_ref, acc_ref) = refs[0:3], refs[3:6], refs[6:9], refs[9:12], refs[12:]
    for i in range(4):
        rows = slice(i * 256, (i + 1) * 256)
        best, weights, total = merge(rows, ms, ls)
        m_ref[rows] = best
        l_ref[rows] = total
        acc_ref[rows] = sum(dot_nn(p[rows], v[...]) * w for p, v, w in zip(ps, vs, weights))


def finish_kernel(at_ref, factor_ref, *refs):
    ms, ls, acc_ref, p_ref, va_ref, vb_ref, keep_ref, share_ref, give_ref = refs[0:2], refs[2:4], *refs[4:]
    b = at_ref[0] * 2 + at_ref[1]
    for chunk, out, place in ((1, give_ref, 0), (3, give_ref, 1), (0, keep_ref, 0), (2, keep_ref, 1)):
        rows = pl.ds(pl.multiple_of((b ^ chunk) * 256, 256), 256)
        _, weights, total = merge(rows, ms, ls)
        far = dot_nn(p_ref[rows, 0:512], va_ref[...]) + dot_nn(p_ref[rows, 512:1024], vb_ref[...])
        acc = acc_ref[rows] * weights[0] + far * weights[1]
        acc = acc / total * factor_ref[rows]
        out[place * 256 : place * 256 + 256] = acc.astype(out.dtype)
        if out is keep_ref:
            share_ref[place * 256 : place * 256 + 256] = acc.astype(BF)


def join_kernel(keep_ref, core_ref, y_ref, both_ref, bv_ref, more_ref, joined_ref, values_ref):
    for n, base in enumerate((bv_ref, more_ref)):
        rows, crossed = slice(n * 256, n * 256 + 256), slice(256 - n * 256, 512 - n * 256)
        joined = keep_ref[rows] + core_ref[rows].astype(F32)
        joined = joined + (y_ref[crossed].astype(F32) + both_ref[crossed].astype(F32))
        if n == 0:
            joined_ref[...] = joined.astype(BF)
        values_ref[rows] = (base[256:512].astype(F32) + joined).astype(BF)


def base_pair_kernel(kv_ref, more_ref, after_ref, out_ref):
    del after_ref
    out_ref[0:256] = kv_ref[0:256]
    out_ref[256:512] = more_ref[0:256]


def base_score_kernel(q_ref, *refs):
    keys, (p_ref, l_ref) = refs[:8], refs[8:]
    blocks = [dot_nt(q_ref[...], k[...]) for k in keys]
    best = jnp.max(functools.reduce(jnp.maximum, blocks), axis=1, keepdims=True)
    total = None
    for n, s in enumerate(blocks):
        p = jnp.exp2((s - best) * SCALE2)
        p_ref[n] = p.astype(BF)
        total = p if total is None else total + p
    l_ref[...] = jnp.sum(total, axis=1, keepdims=True)


def base_value_kernel(at_ref, p_ref, l_ref, joined_ref, *refs):
    values, outs, held = refs[:8], refs[8:12], refs[12]
    acc = None
    for n, v in enumerate(values):
        part = dot_nn(p_ref[n], v[...])
        acc = part if acc is None else acc + part
    held[...] = (acc / l_ref[...]).astype(BF)
    for step, out in enumerate(outs):
        rows = pl.ds(pl.multiple_of(((at_ref[3] + step) & 3) * 64, 64), 64)
        out[0:64] = joined_ref[rows]
        out[64:128] = held[rows]


def home_kernel(at_ref, *refs):
    joined_ref, out_ref = refs[4:]
    for step in range(4):
        head = (at_ref[3] + 4 - step) & 3
        cols = pl.ds(pl.multiple_of(head * DIM, DIM), DIM)
        joined_ref[:, cols] = refs[step][0:64].astype(F32)
        out_ref[:, cols] = refs[step][64:128]


def swap(values, step=0):
    def place(b, c, z):
        return ((b * 2 + c // 2) * 4 + z) * 2 + c % 2

    perm = [
        (place(b, c, z), place(c, b, (z + step) % 4)) for b in range(4) for c in range(4) for z in range(4)
    ]
    return lax.ppermute(values, ("yl", "co", "yh", "zt", "zp"), perm)


def along(axis, values, step):
    return lax.ppermute(values, axis, [(j, (j + step) % 4) for j in range(4)])


def other(values, axis):
    return lax.ppermute(values, axis, [(0, 1), (1, 0)])


def gather_x(pair):
    mine = [pair] + [None] * 3
    for step in (1, 3, 2):
        mine[step] = along("x", pair, step)
    return mine


def gather_core(mine):
    return mine + [other(v, "co") for v in mine]


def shards(ctrl_q, ctrl_k, ctrl_v, codes, base_q, base_k, base_v):
    at = jnp.stack([lax.axis_index(a) for a in ("yl", "co", "x", "zt")]).astype(jnp.int32)

    (packed,) = call(
        pack_kernel,
        [sds((HEADS, 208, DIM))],
        [ctrl_k, ctrl_v, ctrl_q, codes],
        specs=[ANY] * 4,
        out_specs=[ANY],
        vmem=60,
        scratch=[pltpu.VMEM((1, 64), jnp.int32), pltpu.VMEM((HEADS, 208, DIM), BF), pltpu.SemaphoreType.DMA((50,))],
    )
    sent = lax.all_to_all(packed, ("yh", "zt", "zp"), 0, 0, tiled=True)

    parts = call(
        base_pack_kernel,
        [sds((192, DIM))] * 4,
        [at, base_k, base_v, base_q],
        specs=[SM] + [ANY] * 3,
        out_specs=[ANY] * 4,
        scratch=[pltpu.SemaphoreType.DMA((12,))],
    )
    swapped = {step: swap(parts[step], step) for step in (2, 1, 3, 0)}
    parts = [swapped[step] for step in range(4)]
    base_kv, base_quer = call(
        base_unpack_kernel, [sds((512, DIM)), sds((256, DIM))], [at, *parts], specs=[SM] + [VM] * 4
    )
    own_k, own_v, quer, factor = call(
        unpack_kernel,
        [sds((1024, DIM))] * 3 + [sds((1024, 1), F32)],
        [sent, base_quer],
        specs=[VM, ANYWHERE],
    )
    outs = [sds((1024, 1024)), sds((1024, 1), F32), sds((1024, 1), F32)]
    after_k, before_k = along("x", own_k, 1), along("x", own_k, 3)
    *own_score, own_v = call(
        own_score_kernel,
        outs + [sds((1024, DIM))],
        [quer, own_k, own_v],
        specs=[VM, VM, ANYWHERE],
        out_specs=[VM] * 3 + [ANYWHERE],
        vmem=24,
        flops=2 * 1024 * 1024 * 128,
        aliases={2: 3},
    )
    after_v, before_v = along("x", own_v, 1), along("x", own_v, 3)
    far_k = [along("x", after_k[:512], 1), along("x", before_k[512:], 3)]
    far_v = [along("x", after_v[:512], 1), along("x", before_v[512:], 3)]

    more_kv = other(base_kv, "yl")

    scored = [own_score] + [
        call(score_kernel, outs, [quer, k], vmem=24, flops=2 * 1024 * 1024 * 128) for k in (after_k, before_k)
    ]
    ps, ms, ls = zip(*scored)
    m, l, acc = call(
        middle_kernel,
        [sds((1024, 1), F32), sds((1024, 1), F32), sds((1024, DIM), F32)],
        [*ms, *ls, *ps, own_v, after_v, before_v],
        vmem=24,
        flops=3 * 2 * 1024 * 1024 * 128,
    )
    far_p, far_m, far_l = call(score_kernel, outs, [quer, *far_k], vmem=24, flops=2 * 1024 * 1024 * 128)
    keep, share, give = call(
        finish_kernel,
        [sds((512, DIM), F32), sds((512, DIM)), sds((512, DIM))],
        [at, factor, m, far_m, l, far_l, acc, far_p, *far_v],
        specs=[SM] + [VM] * 9,
        vmem=24,
        flops=2 * 1024 * 1024 * 128,
    )

    got_core = other(give, "co")
    got_both = lax.ppermute(give, ("yl", "co"), [(j, j ^ 3) for j in range(4)])
    got_y = other(share, "yl")
    (base_pair,) = call(
        base_pair_kernel, [sds((512, DIM))], [base_kv, more_kv, give], specs=[VM, VM, ANYWHERE]
    )
    base_mine = gather_x(base_pair)
    joined, base_values = call(
        join_kernel,
        [sds((256, DIM)), sds((512, DIM))],
        [keep, got_core, got_y, got_both, base_kv, more_kv],
    )

    base_p, base_l = call(
        base_score_kernel,
        [sds((8, 256, 512)), sds((256, 1), F32)],
        [base_quer, *gather_core(base_mine)],
        vmem=24,
        flops=2 * 256 * 4096 * 128,
    )
    outs = call(
        base_value_kernel,
        [sds((128, DIM))] * 4,
        [at, base_p, base_l, joined, *gather_core(gather_x(base_values))],
        specs=[SM] + [VM] * 11,
        flops=2 * 256 * 4096 * 128,
        scratch=[pltpu.VMEM((256, DIM), BF)],
    )
    result = [None] * 4
    for step in (2, 1, 3, 0):
        result[step] = swap(outs[step], step)
    return call(home_kernel, [sds((64, 512), F32), sds((64, 512))], [at, *result], specs=[SM] + [VM] * 4)


def solution(mesh):
    fine = Mesh(mesh.devices.reshape(2, 2, 4, 2, 4, 2), ("yl", "co", "x", "yh", "zt", "zp"))
    branch, seq = ("yl", "co"), ("x", "yh", "zt", "zp")
    return jax.shard_map(
        shards,
        mesh=fine,
        in_specs=(P(branch, seq, None),) * 3 + (P(branch, seq),) + (P(seq, branch),) * 3,
        out_specs=(P(seq, branch), P(seq, branch)),
        check_vma=False,
    )
```

```python
import functools

import jax
import jax.numpy as jnp
from jax import lax
from jax.experimental import pallas as pl
from jax.experimental.pallas import tpu as pltpu
from jax.sharding import Mesh, PartitionSpec as P

HEADS = 16
DIM = 128
SCALE2 = DIM ** -0.5 * 1.4426950408889634
BF, F32 = jnp.bfloat16, jnp.float32
MIB = 1 << 20
VM = pl.BlockSpec(memory_space=pltpu.VMEM)
SM = pl.BlockSpec(memory_space=pltpu.SMEM)
ANY = pl.BlockSpec(memory_space=pltpu.HBM)
ANYWHERE = pl.BlockSpec(memory_space=pl.ANY)


def call(body, outs, operands, specs=None, out_specs=None, vmem=16, flops=0, scratch=(), aliases={}):
    moved = sum(o.size * o.dtype.itemsize for o in [*operands, *outs])
    return pl.pallas_call(
        body,
        out_shape=outs,
        in_specs=specs or [VM] * len(operands),
        out_specs=out_specs or [VM] * len(outs),
        scratch_shapes=list(scratch),
        input_output_aliases=aliases,
        compiler_params=pltpu.CompilerParams(vmem_limit_bytes=vmem * MIB),
        cost_estimate=pl.CostEstimate(flops=flops, bytes_accessed=moved, transcendentals=0),
    )(*operands)


def sds(shape, dtype=BF):
    return jax.ShapeDtypeStruct(shape, dtype)


def dot_nt(a, b):
    return lax.dot_general(a, b, (((1,), (1,)), ((), ())), preferred_element_type=F32)


def dot_nn(a, b):
    return lax.dot_general(a, b, (((1,), (0,)), ((), ())), preferred_element_type=F32)


def pack_kernel(k_ref, v_ref, q_ref, code_ref, out_ref, code_row, held, sem):
    code = pltpu.make_async_copy(code_ref, code_row, sem.at[48])
    code.start()
    copies = []
    for place in range(HEADS):
        yh, zt, zp = place // 8, place // 2 % 4, place % 2
        head = (yh * 2 + zp) * 4 + zt
        for n, ref in enumerate((k_ref, v_ref, q_ref)):
            source = ref.at[0, :, pl.ds(head * DIM, DIM)]
            target = held.at[place, pl.ds(n * 64, 64)]
            copies.append(pltpu.make_async_copy(source, target, sem.at[place * 3 + n]))
    for copy in copies:
        copy.start()
    code.wait()
    row = jnp.concatenate([code_row[...].astype(F32), jnp.zeros((1, 64), F32)], axis=1)
    held[:, 192:208] = jnp.broadcast_to(row.reshape(1, 1, 128), (HEADS, 16, DIM)).astype(BF)
    outs = []
    for place in range(HEADS):
        for copy in copies[place * 3 : place * 3 + 3]:
            copy.wait()
        outs.append(pltpu.make_async_copy(held.at[place], out_ref.at[place], sem.at[49 + place]))
        outs[-1].start()
    for copy in outs:
        copy.wait()


def base_pack_kernel(at_ref, k_ref, v_ref, q_ref, *refs):
    outs, sem = refs[:4], refs[4]
    copies = []
    for step, out in enumerate(outs):
        head = (at_ref[3] + step) & 3
        for n, ref in enumerate((k_ref, v_ref, q_ref)):
            source = ref.at[:, pl.ds(pl.multiple_of(head * DIM, DIM), DIM)]
            target = out.at[pl.ds(n * 64, 64)]
            copies.append(pltpu.make_async_copy(source, target, sem.at[step * 3 + n]))
    for copy in copies:
        copy.start()
    for copy in copies:
        copy.wait()


def base_unpack_kernel(at_ref, *refs):
    ins, (kv_ref, q_ref) = refs[:4], refs[4:]
    for step, ref in enumerate(ins):
        first = ((at_ref[3] + 4 - step) & 3) * 64
        kv_ref[pl.ds(pl.multiple_of(first, 64), 64)] = ref[0:64]
        kv_ref[pl.ds(pl.multiple_of(256 + first, 64), 64)] = ref[64:128]
        q_ref[pl.ds(pl.multiple_of(first, 64), 64)] = ref[128:192]


def unpack_kernel(in_ref, after_ref, k_ref, v_ref, q_ref, factor_ref):
    del after_ref
    lane = lax.broadcasted_iota(jnp.int32, (64, 128), 1)
    sub = lax.broadcasted_iota(jnp.int32, (64, 128), 0)
    for place in range(16):
        yh, zt, zp = place // 8, place // 2 % 4, place % 2
        t = (yh * 2 + zp) * 4 + zt
        rows = slice(t * 64, (t + 1) * 64)
        k_ref[rows] = in_ref[place, 0:64]
        v_ref[rows] = in_ref[place, 64:128]
        q_ref[rows] = in_ref[place, 128:192]
        code = in_ref[place, 192:208].astype(F32)[0:1]
        code = jnp.broadcast_to(code, (64, 128))
        col = jnp.sum(jnp.where(lane == sub, code, 0.0), axis=1, keepdims=True)
        factor_ref[rows] = col / 16.0


def score_kernel(q_ref, *refs):
    keys, (p_ref, m_ref, l_ref) = refs[:-3], refs[-3:]
    for i in range(8):
        rows = slice(i * 128, (i + 1) * 128)
        parts = [dot_nt(q_ref[rows], k[...]) for k in keys]
        s = jnp.concatenate(parts, axis=1) if len(parts) > 1 else parts[0]
        m = jnp.max(s, axis=1, keepdims=True)
        p = jnp.exp2((s - m) * SCALE2)
        m_ref[rows] = m
        l_ref[rows] = jnp.sum(p, axis=1, keepdims=True)
        p_ref[rows] = p.astype(BF)


def own_score_kernel(q_ref, k_ref, v_ref, p_ref, m_ref, l_ref, same_v_ref):
    del v_ref, same_v_ref
    score_kernel(q_ref, k_ref, p_ref, m_ref, l_ref)


def merge(rows, ms, ls):
    m = [r[rows] for r in ms]
    best = functools.reduce(jnp.maximum, m)
    weights = [jnp.exp2((x - best) * SCALE2) for x in m]
    return best, weights, sum(w * l[rows] for w, l in zip(weights, ls))


def middle_kernel(*refs):
    ms, ls, ps, vs, (m_ref, l_ref, acc_ref) = refs[0:3], refs[3:6], refs[6:9], refs[9:12], refs[12:]
    for i in range(8):
        rows = slice(i * 128, (i + 1) * 128)
        best, weights, total = merge(rows, ms, ls)
        m_ref[rows] = best
        l_ref[rows] = total
        acc_ref[rows] = sum(dot_nn(p[rows], v[...]) * w for p, v, w in zip(ps, vs, weights))


def finish_kernel(at_ref, factor_ref, *refs):
    ms, ls, acc_ref, p_ref, va_ref, vb_ref, keep_ref, share_ref, give_ref = refs[0:2], refs[2:4], *refs[4:]
    b = at_ref[0] * 2 + at_ref[1]
    for chunk, out, place in ((1, give_ref, 0), (3, give_ref, 1), (0, keep_ref, 0), (2, keep_ref, 1)):
        rows = pl.ds(pl.multiple_of((b ^ chunk) * 256, 256), 256)
        _, weights, total = merge(rows, ms, ls)
        far = dot_nn(p_ref[rows, 0:512], va_ref[...]) + dot_nn(p_ref[rows, 512:1024], vb_ref[...])
        acc = acc_ref[rows] * weights[0] + far * weights[1]
        acc = acc / total * factor_ref[rows]
        out[place * 256 : place * 256 + 256] = acc.astype(out.dtype)
        if out is keep_ref:
            share_ref[place * 256 : place * 256 + 256] = acc.astype(BF)


def join_kernel(keep_ref, core_ref, y_ref, both_ref, bv_ref, more_ref, joined_ref, values_ref):
    for n, base in enumerate((bv_ref, more_ref)):
        rows, crossed = slice(n * 256, n * 256 + 256), slice(256 - n * 256, 512 - n * 256)
        joined = keep_ref[rows] + core_ref[rows].astype(F32)
        joined = joined + (y_ref[crossed].astype(F32) + both_ref[crossed].astype(F32))
        if n == 0:
            joined_ref[...] = joined.astype(BF)
        values_ref[rows] = (base[256:512].astype(F32) + joined).astype(BF)


def base_pair_kernel(kv_ref, more_ref, after_ref, out_ref):
    del after_ref
    out_ref[0:256] = kv_ref[0:256]
    out_ref[256:512] = more_ref[0:256]


def base_score_kernel(q_ref, *refs):
    keys, (p_ref, l_ref) = refs[:8], refs[8:]
    blocks = [dot_nt(q_ref[...], k[...]) for k in keys]
    best = jnp.max(functools.reduce(jnp.maximum, blocks), axis=1, keepdims=True)
    total = None
    for n, s in enumerate(blocks):
        p = jnp.exp2((s - best) * SCALE2)
        p_ref[n] = p.astype(BF)
        total = p if total is None else total + p
    l_ref[...] = jnp.sum(total, axis=1, keepdims=True)


def base_value_kernel(at_ref, p_ref, l_ref, joined_ref, *refs):
    values, outs, held = refs[:8], refs[8:12], refs[12]
    acc = None
    for n, v in enumerate(values):
        part = dot_nn(p_ref[n], v[...])
        acc = part if acc is None else acc + part
    held[...] = (acc / l_ref[...]).astype(BF)
    for step, out in enumerate(outs):
        rows = pl.ds(pl.multiple_of(((at_ref[3] + step) & 3) * 64, 64), 64)
        out[0:64] = joined_ref[rows]
        out[64:128] = held[rows]


def home_kernel(at_ref, *refs):
    joined_ref, out_ref = refs[4:]
    for step in range(4):
        head = (at_ref[3] + 4 - step) & 3
        cols = pl.ds(pl.multiple_of(head * DIM, DIM), DIM)
        joined_ref[:, cols] = refs[step][0:64].astype(F32)
        out_ref[:, cols] = refs[step][64:128]


def swap(values, step=0):
    def place(b, c, z):
        return ((b * 2 + c // 2) * 4 + z) * 2 + c % 2

    perm = [
        (place(b, c, z), place(c, b, (z + step) % 4)) for b in range(4) for c in range(4) for z in range(4)
    ]
    return lax.ppermute(values, ("yl", "co", "yh", "zt", "zp"), perm)


def along(axis, values, step):
    return lax.ppermute(values, axis, [(j, (j + step) % 4) for j in range(4)])


def other(values, axis):
    return lax.ppermute(values, axis, [(0, 1), (1, 0)])


def gather_x(pair):
    mine = [pair] + [None] * 3
    for step in (1, 3, 2):
        mine[step] = along("x", pair, step)
    return mine


def gather_core(mine):
    return mine + [other(v, "co") for v in mine]


def shards(ctrl_q, ctrl_k, ctrl_v, codes, base_q, base_k, base_v):
    at = jnp.stack([lax.axis_index(a) for a in ("yl", "co", "x", "zt")]).astype(jnp.int32)

    (packed,) = call(
        pack_kernel,
        [sds((HEADS, 208, DIM))],
        [ctrl_k, ctrl_v, ctrl_q, codes],
        specs=[ANY] * 4,
        out_specs=[ANY],
        vmem=60,
        scratch=[pltpu.VMEM((1, 64), jnp.int32), pltpu.VMEM((HEADS, 208, DIM), BF), pltpu.SemaphoreType.DMA((65,))],
    )
    sent = lax.all_to_all(packed, ("yh", "zt", "zp"), 0, 0, tiled=True)

    parts = call(
        base_pack_kernel,
        [sds((192, DIM))] * 4,
        [at, base_k, base_v, base_q],
        specs=[SM] + [ANY] * 3,
        out_specs=[ANY] * 4,
        scratch=[pltpu.SemaphoreType.DMA((12,))],
    )
    swapped = {step: swap(parts[step], step) for step in (2, 1, 3, 0)}
    parts = [swapped[step] for step in range(4)]
    base_kv, base_quer = call(
        base_unpack_kernel, [sds((512, DIM)), sds((256, DIM))], [at, *parts], specs=[SM] + [VM] * 4
    )
    own_k, own_v, quer, factor = call(
        unpack_kernel,
        [sds((1024, DIM))] * 3 + [sds((1024, 1), F32)],
        [sent, base_quer],
        specs=[VM, ANYWHERE],
    )
    outs = [sds((1024, 1024)), sds((1024, 1), F32), sds((1024, 1), F32)]
    after_k, before_k = along("x", own_k, 1), along("x", own_k, 3)
    *own_score, own_v = call(
        own_score_kernel,
        outs + [sds((1024, DIM))],
        [quer, own_k, own_v],
        specs=[VM, VM, ANYWHERE],
        out_specs=[VM] * 3 + [ANYWHERE],
        vmem=24,
        flops=2 * 1024 * 1024 * 128,
        aliases={2: 3},
    )
    after_v, before_v = along("x", own_v, 1), along("x", own_v, 3)
    far_k = [along("x", after_k[:512], 1), along("x", before_k[512:], 3)]
    far_v = [along("x", after_v[:512], 1), along("x", before_v[512:], 3)]

    more_kv = other(base_kv, "yl")

    scored = [own_score] + [
        call(score_kernel, outs, [quer, k], vmem=24, flops=2 * 1024 * 1024 * 128) for k in (after_k, before_k)
    ]
    ps, ms, ls = zip(*scored)
    m, l, acc = call(
        middle_kernel,
        [sds((1024, 1), F32), sds((1024, 1), F32), sds((1024, DIM), F32)],
        [*ms, *ls, *ps, own_v, after_v, before_v],
        vmem=24,
        flops=3 * 2 * 1024 * 1024 * 128,
    )
    far_p, far_m, far_l = call(score_kernel, outs, [quer, *far_k], vmem=24, flops=2 * 1024 * 1024 * 128)
    keep, share, give = call(
        finish_kernel,
        [sds((512, DIM), F32), sds((512, DIM)), sds((512, DIM))],
        [at, factor, m, far_m, l, far_l, acc, far_p, *far_v],
        specs=[SM] + [VM] * 9,
        vmem=24,
        flops=2 * 1024 * 1024 * 128,
    )

    got_core = other(give, "co")
    got_both = lax.ppermute(give, ("yl", "co"), [(j, j ^ 3) for j in range(4)])
    got_y = other(share, "yl")
    (base_pair,) = call(
        base_pair_kernel, [sds((512, DIM))], [base_kv, more_kv, give], specs=[VM, VM, ANYWHERE]
    )
    base_mine = gather_x(base_pair)
    joined, base_values = call(
        join_kernel,
        [sds((256, DIM)), sds((512, DIM))],
        [keep, got_core, got_y, got_both, base_kv, more_kv],
    )

    base_p, base_l = call(
        base_score_kernel,
        [sds((8, 256, 512)), sds((256, 1), F32)],
        [base_quer, *gather_core(base_mine)],
        vmem=24,
        flops=2 * 256 * 4096 * 128,
    )
    outs = call(
        base_value_kernel,
        [sds((128, DIM))] * 4,
        [at, base_p, base_l, joined, *gather_core(gather_x(base_values))],
        specs=[SM] + [VM] * 11,
        flops=2 * 256 * 4096 * 128,
        scratch=[pltpu.VMEM((256, DIM), BF)],
    )
    result = [None] * 4
    for step in (2, 1, 3, 0):
        result[step] = swap(outs[step], step)
    return call(home_kernel, [sds((64, 512), F32), sds((64, 512))], [at, *result], specs=[SM] + [VM] * 4)


def solution(mesh):
    fine = Mesh(mesh.devices.reshape(2, 2, 4, 2, 4, 2), ("yl", "co", "x", "yh", "zt", "zp"))
    branch, seq = ("yl", "co"), ("x", "yh", "zt", "zp")
    return jax.shard_map(
        shards,
        mesh=fine,
        in_specs=(P(branch, seq, None),) * 3 + (P(branch, seq),) + (P(seq, branch),) * 3,
        out_specs=(P(seq, branch), P(seq, branch)),
        check_vma=False,
    )
```
